32 devices in a mesh: groups: 2 (over y), tm: 16 (over z, x, core).
Axes of the slice: x: 2, y: 2, z: 4, core: 2. Of those that a mesh axis runs over, the one named last changes fastest.
Arguments:
- voltages: bfloat16 [256, 256, 2, 188], P(None, ('groups', 'tm')), parts along dimension 1, as said below
- off_starts: int32 [16], P('groups'), parts along dimension 0, may hold values from 0 to 124, as said below
- pointing: int32 [36], replicated, may hold values from 0 to 2047, as said below
- patterns: bfloat16 [2, 188, 2048], P(None, None, 'tm'), may hold values from -0.3125 to 0.3125
Outputs:
- beam_weights: bfloat16 [512, 2, 6768], P(('groups', 'tm')), parts along dimension 0
- beam_maps: float32 [512, 36, 2048], P('groups', None, 'tm'), parts along dimension 0
The draws below stay inside these ranges and needn't reach their ends.
There are 2 independent parts, one for each index of `groups`. The reference program is written for one: setup_inputs(seed, part) draws one part's arguments, and reference() takes and returns one part's arrays. A program takes and returns all parts, laid end to end along the dimension named above; an argument that names none is the same for every part. Nothing has to cross between parts.
Inputs may be any that keep to these rules, and one draw needn't show every extreme that they name: Complex port voltages: thermal noise whose power differs between ports and grows along time, plus sky signals common to the ports. `off_starts`: each of the 8 off-source ranges covers 4 samples from this start; ranges may intersect. `pointing`: several beams may point at the same pixel.
All inputs are finite; a program needn't handle non-finite values.
Results may differ from the reference program's by a relative error of at most 0.0034.
Values may be sent and summed in bfloat16 or wider, within the bound.
A program may use at most 64 MiB of HBM per device.

```python
import math
import jax
import jax.numpy as jnp
from jax import lax

P_SIZE = 188
B = 36
CH = 256
ITERS = 20
RANGES = 8
TIME = 128
PIX = 2048
OFF_LEN = 4


def draw_voltages(key, part):
    subkeys = jax.random.split(jax.random.fold_in(key, 11), 4)
    thermal = jax.random.truncated_normal(subkeys[0], -5.0, 5.0, (CH, TIME, 2, P_SIZE), jnp.float32)
    port_amp = jnp.exp(jax.random.uniform(subkeys[1], (CH, 1, 1, P_SIZE), jnp.float32, 0.0, math.log(3.0)))
    gain_scale = 0.25
    drift = jnp.sqrt(1.0 + 2.0 * jnp.arange(TIME, dtype=jnp.float32) / TIME)
    sources = jax.random.normal(subkeys[2], (CH, TIME, 2, 3), jnp.float32)
    port_gains = gain_scale * jax.random.normal(subkeys[3], (CH, 3, 2, P_SIZE), jnp.float32)
    signal_real = jnp.einsum('ctk,ckp->ctp', sources[:, :, 0], port_gains[:, :, 0]) - jnp.einsum('ctk,ckp->ctp', sources[:, :, 1], port_gains[:, :, 1])
    signal_imag = jnp.einsum('ctk,ckp->ctp', sources[:, :, 0], port_gains[:, :, 1]) + jnp.einsum('ctk,ckp->ctp', sources[:, :, 1], port_gains[:, :, 0])
    return (thermal * port_amp * drift[None, :, None, None] + jnp.stack([signal_real, signal_imag], axis=2)).astype(jnp.bfloat16)


def draw_off_starts(key, part):
    drawn = jax.random.randint(jax.random.fold_in(key, 23), (RANGES,), 0, TIME - OFF_LEN + 1, dtype=jnp.int32)
    ranks = jnp.arange(RANGES, dtype=jnp.int32)
    return jnp.where(ranks == 0, 0, jnp.where(ranks == 1, TIME - OFF_LEN, drawn)).astype(jnp.int32)


def draw_pointing(key, part):
    drawn = jax.random.randint(jax.random.fold_in(key, 37), (B,), 0, PIX, dtype=jnp.int32)
    ranks = jnp.arange(B, dtype=jnp.int32)
    return jnp.where(ranks == 0, PIX - 1, jnp.where(ranks == 1, 0, drawn)).astype(jnp.int32)


def levels(rng, extent, cuts, smallest, largest):
    def one(dim, blocks):
        heights = jax.random.uniform(jax.random.fold_in(jax.random.fold_in(rng, 6), dim), (blocks,), jnp.float32, smallest / len(cuts), largest / len(cuts))
        return jnp.repeat(jnp.exp(heights), extent[dim] // blocks).reshape((-1,) + (1,) * (len(extent) - dim - 1))

    loudness = one(*cuts[0])
    for cut in cuts[1:]:
        loudness = loudness * one(*cut)
    return loudness


def centred(rng, extent, spread, bound, cuts=(), kind=jnp.bfloat16):
    array = jax.random.normal(rng, extent, jnp.float32) * spread
    if len(cuts) > 0:
        array = levels(rng, extent, cuts, -0.22, 0.18) * array
    return jnp.clip(array, min=-bound, max=bound).astype(kind)


def setup_inputs(seed: int = 0, part: int = 0) -> dict:
    key_list = jax.random.split(jax.random.key(seed), 5)
    part_splits = jax.random.split(jax.random.fold_in(key_list[4], part), 5)
    return {
        "voltages": draw_voltages(jax.random.fold_in(jax.random.fold_in(key_list[4], part), 71), part),
        "off_starts": draw_off_starts(jax.random.fold_in(jax.random.fold_in(key_list[4], part), 71), part),
        "pointing": draw_pointing(jax.random.fold_in(key_list[4], 71), part),
        "patterns": centred(key_list[3], (2, P_SIZE, PIX), (2 * P_SIZE) ** -0.5, 0.3125, ((2, 16),)),
    }


highest = lax.Precision.HIGHEST

def off_flags(starts):
    moments = jnp.arange(TIME, dtype=jnp.int32)
    inside = (moments[None, :] >= starts[:, None]) & (moments[None, :] < starts[:, None] + OFF_LEN)
    return jnp.any(inside, axis=0)

def beam_power(weights, patterns):
    real_rows = jnp.concatenate([weights[:, 0], weights[:, 1]], axis=-1)
    imag_rows = jnp.concatenate([-weights[:, 1], weights[:, 0]], axis=-1)
    rows_all = jnp.stack([real_rows, imag_rows], axis=2).reshape(-1, 2 * P_SIZE)
    response = jnp.dot(rows_all, patterns.reshape(2 * P_SIZE, -1), preferred_element_type=jnp.float32)
    response = response.reshape(weights.shape[0], weights.shape[2], 2, -1)
    return response[:, :, 0] * response[:, :, 0] + response[:, :, 1] * response[:, :, 1]

def reference(voltages, off_starts, pointing, patterns):
    is_off = off_flags(off_starts)
    off_count = jnp.sum(is_off.astype(jnp.float32))

    def channel_stats(channel_volts):
        samples = channel_volts.reshape(TIME, 2 * P_SIZE)
        on_source = jnp.where(is_off[:, None], jnp.zeros_like(samples), samples)
        products = lax.dot_general(on_source, samples, (((0,), (0,)), ((), ())), preferred_element_type=jnp.float32)
        corr_real = products[:P_SIZE, :P_SIZE] + products[P_SIZE:, P_SIZE:]
        corr_imag = products[P_SIZE:, :P_SIZE] - products[:P_SIZE, P_SIZE:]
        widened = samples.astype(jnp.float32)
        powers = lax.optimization_barrier(jnp.sum(jnp.where(is_off[:, None], widened * widened, jnp.float32(0.0)), axis=0))
        return (jnp.stack([corr_real, corr_imag]), powers[:P_SIZE] + powers[P_SIZE:])
    correlation, noise_sums = lax.map(channel_stats, voltages)
    noise_power = noise_sums / off_count + 1e-06
    scales = 1.0 / jnp.sqrt(noise_power)
    white_real = correlation[:, 0] * scales[:, :, None] * scales[:, None, :]
    white_imag = correlation[:, 1] * scales[:, :, None] * scales[:, None, :]
    steering = jnp.take(patterns, pointing, axis=2).astype(jnp.float32)
    steer_real = steering[0][None]
    steer_imag = steering[1][None]

    def apply_white(matrix, vector):
        return jnp.einsum('cij,cjb->cib', matrix, vector, precision=highest)

    def power_turn(counter, state_pair):
        beam_real, beam_imag = state_pair
        conj_real = steer_real * beam_real + steer_imag * beam_imag
        conj_imag = steer_real * beam_imag - steer_imag * beam_real
        mixed_real = apply_white(white_real, conj_real) - apply_white(white_imag, conj_imag)
        mixed_imag = apply_white(white_real, conj_imag) + apply_white(white_imag, conj_real)
        image_real = steer_real * mixed_real - steer_imag * mixed_imag
        image_imag = steer_real * mixed_imag + steer_imag * mixed_real
        mean_square = (lax.optimization_barrier(jnp.sum(image_real * image_real, axis=1)) + lax.optimization_barrier(jnp.sum(image_imag * image_imag, axis=1))) / (2 * P_SIZE)
        factor = 1.0 / jnp.sqrt(mean_square + 1e-06)
        return (image_real * factor[:, None, :], image_imag * factor[:, None, :])
    initial = (jnp.broadcast_to(steer_real, (CH, P_SIZE, B)), jnp.broadcast_to(steer_imag, (CH, P_SIZE, B)))
    beam_real, beam_imag = lax.fori_loop(0, ITERS, power_turn, initial)
    weight_real = beam_real * scales[:, :, None]
    weight_imag = beam_imag * scales[:, :, None]
    weights = jnp.stack([weight_real, weight_imag], axis=1).transpose(0, 1, 3, 2).astype(jnp.bfloat16)
    beam_weights = weights.reshape(CH, 2, B * P_SIZE)
    beam_maps = lax.map(lambda single: beam_power(single, patterns)[0], weights[:, None])
    return (beam_weights, beam_maps)
```

```python
import functools
import jax
import jax.numpy as jnp
from jax import lax
from jax.experimental import pallas as pl
from jax.experimental.pallas import tpu as pltpu
from jax.sharding import PartitionSpec as P

ITERS = 20
ROUGH = 0


def off_flags(moments, starts, range_len):
    inside = (moments[None, :] >= starts[:, None]) & (
        moments[None, :] < starts[:, None] + range_len
    )
    return jnp.any(inside, axis=0)


def split_two(value):
    high = value.astype(jnp.bfloat16)
    return high, (value - high.astype(jnp.float32)).astype(jnp.bfloat16)


def dot32(a, b):
    return jnp.dot(a, b, preferred_element_type=jnp.float32)


def power_kernel(volt_ref, mask_ref, count_ref, steer_ref, out_ref, real_hi, real_lo, imag_hi, imag_lo):
    senders, chans, rows_dev, ports = volt_ref.shape
    rows = senders * rows_dev
    beams = steer_ref.shape[0] // 2
    chunk = 256
    steer_real = steer_ref[:beams]
    steer_imag = steer_ref[beams:]
    gain = steer_real * steer_real + steer_imag * steer_imag
    row_id = lax.broadcasted_iota(jnp.int32, (chunk, chunk), 0)
    col_id = lax.broadcasted_iota(jnp.int32, (chunk, chunk), 1)
    even = lax.rem(row_id, 2) == 0
    turn = jnp.where(
        even & (col_id == row_id + 1), 1.0, jnp.where((~even) & (col_id == row_id - 1), -1.0, 0.0)
    ).astype(jnp.bfloat16)
    inverse_noise = []
    for c in range(chans):
        samples = volt_ref[:, c].reshape(rows, ports)
        mask = mask_ref[...]
        on_source = samples * mask
        wide = samples.astype(jnp.float32)
        off_power = jnp.sum(
            wide * wide * (1.0 - mask.astype(jnp.float32)), axis=0, keepdims=True
        )
        inverse_noise.append(1.0 / (off_power / count_ref[...] + 1e-06))
        turned = [
            dot32(turn, on_source[k : k + chunk]).astype(jnp.bfloat16)
            for k in range(0, rows, chunk)
        ]
        turned = turned[0] if len(turned) == 1 else jnp.concatenate(turned, axis=0)
        dims = (((0,), (0,)), ((), ()))
        corr_real = lax.dot_general(on_source, samples, dims, preferred_element_type=jnp.float32)
        corr_imag = lax.dot_general(turned, samples, dims, preferred_element_type=jnp.float32)
        real_hi[c], real_lo[c] = split_two(corr_real)
        imag_hi[c], imag_lo[c] = split_two(corr_imag)

    def mix(c, state, rough):
        if rough:
            high = state.astype(jnp.bfloat16)
            by_real = dot32(high, real_hi[c])
            by_imag = dot32(high, imag_hi[c])
        else:
            high, low = split_two(state)
            both = jnp.concatenate([high, low], axis=0)
            by_real = dot32(both, real_hi[c])
            by_imag = dot32(both, imag_hi[c])
            by_real = by_real[: 2 * beams] + by_real[2 * beams :] + dot32(high, real_lo[c])
            by_imag = by_imag[: 2 * beams] + by_imag[2 * beams :] + dot32(high, imag_lo[c])
        return by_real[:beams] + by_imag[beams:], by_real[beams:] - by_imag[:beams]

    weighting = [gain * inv for inv in inverse_noise]

    def power_turn(rough, counter, states):
        new_states = []
        for c in range(chans):
            mixed_real, mixed_imag = mix(c, states[c], rough)
            next_real = weighting[c] * mixed_real
            next_imag = weighting[c] * mixed_imag
            total = jnp.sum(
                next_real * mixed_real + next_imag * mixed_imag, axis=1, keepdims=True
            )
            factor = lax.rsqrt(total / (2 * ports) + 1e-06)
            new_states.append(jnp.concatenate([next_real * factor, next_imag * factor], axis=0))
        return tuple(new_states)

    states = tuple(
        jnp.concatenate([gain * jnp.sqrt(inv), jnp.zeros_like(gain)], axis=0)
        for inv in inverse_noise
    )
    if ROUGH > 0:
        states = lax.fori_loop(0, ROUGH, functools.partial(power_turn, True), states)
    states = lax.fori_loop(ROUGH, ITERS - 1, functools.partial(power_turn, False), states)
    for c in range(chans):
        mixed_real, mixed_imag = mix(c, states[c], False)
        total = jnp.sum(
            weighting[c] * mixed_real * mixed_real + weighting[c] * mixed_imag * mixed_imag,
            axis=1,
            keepdims=True,
        )
        factor = lax.rsqrt(total / (2 * ports) + 1e-06) * inverse_noise[c]
        weight_real = (steer_real * mixed_real - steer_imag * mixed_imag) * factor
        weight_imag = (steer_real * mixed_imag + steer_imag * mixed_real) * factor
        out_ref[c] = jnp.concatenate([weight_real, weight_imag], axis=0).astype(jnp.bfloat16)


def power_weights(arrived, mask, count, steering):
    senders, chans, rows_dev, ports = arrived.shape
    beams2 = steering.shape[0]
    work = chans * ITERS * 2 * ports * ports * 3 * beams2 * 2
    return pl.pallas_call(
        power_kernel,
        out_shape=jax.ShapeDtypeStruct((chans, beams2, ports), jnp.bfloat16),
        in_specs=[pl.BlockSpec(memory_space=pltpu.VMEM)] * 4,
        out_specs=pl.BlockSpec(memory_space=pltpu.VMEM),
        scratch_shapes=[pltpu.VMEM((chans, ports, ports), jnp.bfloat16)] * 4,
        compiler_params=pltpu.CompilerParams(vmem_limit_bytes=32 * 1024 * 1024),
        cost_estimate=pl.CostEstimate(
            flops=10 * work, bytes_accessed=2 * arrived.size, transcendentals=0
        ),
    )(arrived, mask, count, steering)


def map_kernel(beams, weights_ref, pattern_ref, *rest):
    out_ref = rest[-1]
    _, chans, beams2, ports = weights_ref.shape
    padded = beams2 // 2
    pixels = pattern_ref.shape[1] // 2
    flat = weights_ref[0].reshape(chans * beams2, ports)
    response = dot32(flat, pattern_ref[...]).reshape(chans, 2, padded, 2 * pixels)
    real = response[:, 0, :, :pixels] + response[:, 1, :, pixels:]
    imag = response[:, 0, :, pixels:] - response[:, 1, :, :pixels]
    out_ref[0] = (real * real + imag * imag)[:, :beams]


def beam_power(gathered, patterns, part, parts, beams, before):
    senders, chans, beams2, ports = gathered.shape
    pixels = patterns.shape[1] // 2
    in_specs = [
        pl.BlockSpec((1, chans, beams2, ports), lambda i: (i, 0, 0, 0)),
        pl.BlockSpec((ports, 2 * pixels), lambda i: (0, 0)),
    ]
    operands = [gathered, patterns]
    aliases = {}
    if before is not None:
        in_specs.append(pl.BlockSpec(memory_space=pl.ANY))
        operands.append(before)
        aliases = {2: 0}
    return pl.pallas_call(
        functools.partial(map_kernel, beams),
        grid=(senders,),
        out_shape=jax.ShapeDtypeStruct((senders, parts * chans, beams, pixels), jnp.float32),
        in_specs=in_specs,
        out_specs=pl.BlockSpec((1, chans, beams, pixels), lambda i: (i, part, 0, 0)),
        input_output_aliases=aliases,
        compiler_params=pltpu.CompilerParams(vmem_limit_bytes=32 * 1024 * 1024),
    )(*operands)


def on_device(voltages, off_starts, pointing, patterns):
    devices = lax.axis_size("tm")
    position = lax.axis_index("tm")
    channels, samples_dev, _, ports = voltages.shape
    beams = pointing.shape[0]
    padded = -(-beams // 8) * 8
    per_dev = channels // devices
    parts = 4 if per_dev % 4 == 0 else per_dev
    chans = per_dev // parts
    rows_dev = 2 * samples_dev
    total_time = samples_dev * devices
    off_span = max(4, total_time // 32)
    is_off = off_flags(jnp.arange(total_time, dtype=jnp.int32), off_starts, off_span)
    off_count = jnp.sum(is_off.astype(jnp.float32))
    count = jnp.broadcast_to(off_count, (1, ports))
    mask = jnp.broadcast_to(
        jnp.repeat(~is_off, 2)[:, None], (2 * total_time, ports)
    ).astype(jnp.bfloat16)
    pixels = patterns.shape[2]
    pixel_ids = position * pixels + jnp.arange(pixels, dtype=jnp.int32)
    wanted = jnp.pad(pointing, (0, padded - beams), constant_values=-1)
    selector = (wanted[:, None] == pixel_ids[None, :]).astype(jnp.bfloat16)
    picked = jnp.einsum("rpx,bx->rbp", patterns, selector, preferred_element_type=jnp.float32)
    picked = picked.astype(jnp.bfloat16).reshape(1, 2 * padded, ports)
    spread = jnp.broadcast_to(picked, (devices, 2 * padded, ports))
    spread = lax.all_to_all(spread, "tm", split_axis=0, concat_axis=0, tiled=True)
    steering = jnp.sum(spread.astype(jnp.float32), axis=0)
    blocks = voltages.reshape(devices, parts, chans, rows_dev, ports)
    pattern_rows = jnp.concatenate([patterns[0], patterns[1]], axis=1)
    arrived = [
        lax.all_to_all(blocks[:, k], "tm", split_axis=0, concat_axis=0, tiled=True)
        for k in range(parts)
    ]
    weights = [power_weights(a, mask, count, steering) for a in arrived]
    gathered = [lax.all_gather(w, "tm", axis=0) for w in weights]
    maps = None
    for k in range(parts):
        maps = beam_power(gathered[k], pattern_rows, k, parts, beams, maps)
    flat = jnp.stack(weights).reshape(per_dev, 2, padded, ports)[:, :, :beams]
    return (
        flat.reshape(per_dev, 2, beams * ports),
        maps.reshape(channels, beams, pixels),
    )


def solution(mesh):
    in_specs = (P(None, ("groups", "tm"), None, None), P("groups"), P(), P(None, None, "tm"))
    out_specs = (P(("groups", "tm"), None, None), P("groups", None, "tm"))
    return jax.shard_map(
        on_device, mesh=mesh, in_specs=in_specs, out_specs=out_specs, check_vma=False
    )
```

```python
import functools
import jax
import jax.numpy as jnp
from jax import lax
from jax.experimental import pallas as pl
from jax.experimental.pallas import tpu as pltpu
from jax.sharding import PartitionSpec as P

ITERS = 20
MESH = pl.DeviceIdType.MESH


def off_flags(moments, starts, range_len):
    inside = (moments[None, :] >= starts[:, None]) & (
        moments[None, :] < starts[:, None] + range_len
    )
    return jnp.any(inside, axis=0)


def split_two(value):
    high = value.astype(jnp.bfloat16)
    return high, (value - high.astype(jnp.float32)).astype(jnp.bfloat16)


def dot32(a, b):
    return jnp.dot(a, b, preferred_element_type=jnp.float32)


def correlate(volt_ref, part, c, mask, count):
    senders, rows_dev, width = volt_ref.shape[1:]
    ports = width // 2
    samples_dev = mask.shape[0] // senders
    wide = volt_ref[part].astype(jnp.float32)
    wide = wide[:, c * samples_dev : (c + 1) * samples_dev].reshape(senders * samples_dev, width)
    first, second = wide[:, :ports], wide[:, ports:]
    on_first, on_second = first * mask, second * mask
    power = (first * first + second * second) * (1.0 - mask)
    noise_power = jnp.sum(power, axis=0, keepdims=True) / count + 1e-06
    pair = jnp.concatenate([first, second], axis=0).astype(jnp.bfloat16)
    on_pair = jnp.concatenate([on_first, on_second], axis=0).astype(jnp.bfloat16)
    turned = jnp.concatenate([on_second, -on_first], axis=0).astype(jnp.bfloat16)
    dims = (((0,), (0,)), ((), ()))
    corr_real = lax.dot_general(on_pair, pair, dims, preferred_element_type=jnp.float32)
    corr_imag = lax.dot_general(turned, pair, dims, preferred_element_type=jnp.float32)
    return corr_real, corr_imag, 1.0 / noise_power


def compute_part(part, volt_ref, mask_ref, count_ref, steer_ref, out_ref, mats):
    real_hi, real_lo, imag_hi, imag_lo = mats
    chans = real_hi.shape[0]
    ports = real_hi.shape[1]
    beams = steer_ref.shape[0] // 2
    steer_real = steer_ref[:beams]
    steer_imag = steer_ref[beams:]
    gain = steer_real * steer_real + steer_imag * steer_imag
    inverse_noise = []
    for c in range(chans):
        corr_real, corr_imag, inverse = correlate(
            volt_ref, part, c, mask_ref[...], count_ref[...]
        )
        inverse_noise.append(inverse)
        real_hi[c], real_lo[c] = split_two(corr_real)
        imag_hi[c], imag_lo[c] = split_two(corr_imag)

    def mix(c, state):
        high, low = split_two(state)
        both = jnp.concatenate([high, low], axis=0)
        by_real = dot32(both, real_hi[c])
        by_imag = dot32(both, imag_hi[c])
        by_real = by_real[: 2 * beams] + by_real[2 * beams :] + dot32(high, real_lo[c])
        by_imag = by_imag[: 2 * beams] + by_imag[2 * beams :] + dot32(high, imag_lo[c])
        return by_real[:beams] + by_imag[beams:], by_real[beams:] - by_imag[:beams]

    weighting = [gain * inv for inv in inverse_noise]

    def power_turn(counter, states):
        new_states = []
        for c in range(chans):
            mixed_real, mixed_imag = mix(c, states[c])
            next_real = weighting[c] * mixed_real
            next_imag = weighting[c] * mixed_imag
            total = jnp.sum(
                next_real * mixed_real + next_imag * mixed_imag, axis=1, keepdims=True
            )
            factor = lax.rsqrt(total / (2 * ports) + 1e-06)
            new_states.append(jnp.concatenate([next_real * factor, next_imag * factor], axis=0))
        return tuple(new_states)

    states = tuple(
        jnp.concatenate([gain * jnp.sqrt(inv), jnp.zeros_like(gain)], axis=0)
        for inv in inverse_noise
    )
    states = lax.fori_loop(0, ITERS - 1, power_turn, states)
    results = []
    for c in range(chans):
        mixed_real, mixed_imag = mix(c, states[c])
        total = jnp.sum(
            weighting[c] * mixed_real * mixed_real + weighting[c] * mixed_imag * mixed_imag,
            axis=1,
            keepdims=True,
        )
        factor = lax.rsqrt(total / (2 * ports) + 1e-06) * inverse_noise[c]
        weight_real = (steer_real * mixed_real - steer_imag * mixed_imag) * factor
        weight_imag = (steer_real * mixed_imag + steer_imag * mixed_real) * factor
        results.append(jnp.concatenate([weight_real, weight_imag], axis=1))
    out_ref[part] = jnp.concatenate(results, axis=0).astype(jnp.bfloat16)


def exchange_kernel(
    dims, blocks_ref, pick_ref, mask_ref, count_ref, gathered_ref, own_ref,
    arrived, slots, partial, steer, real_hi, real_lo, imag_hi, imag_lo,
    volt_send, volt_recv, steer_send, steer_recv,
    z_send, z_recv, x_send, x_recv, core_send, core_recv, place_sem,
):
    depth, width, cores = dims
    devices = depth * width * cores
    parts = arrived.shape[0]
    me = lax.axis_index("tm")
    my_core = lax.rem(me, cores)
    my_x = lax.rem(me // cores, width)
    my_z = me // (cores * width)

    def device(z, x, core):
        return {"tm": (z * width + x) * cores + core}

    def remote(src, dst, send, recv, target):
        return pltpu.make_async_remote_copy(
            src_ref=src, dst_ref=dst, send_sem=send, recv_sem=recv,
            device_id=target, device_id_type=MESH,
        )

    def take(ref, sem):
        pltpu.make_async_copy(ref, ref, sem).wait()

    barrier = pltpu.get_barrier_semaphore()

    @pl.loop(1, devices)
    def _(step):
        pl.semaphore_signal(
            barrier, inc=1, device_id={"tm": lax.rem(me + step, devices)}, device_id_type=MESH
        )

    pl.semaphore_wait(barrier, devices - 1)

    def start_volts(part):
        @pl.loop(1, devices)
        def _(step):
            target = lax.rem(me + step, devices)
            remote(
                blocks_ref.at[target, part], arrived.at[part, me],
                volt_send.at[part], volt_recv.at[part], {"tm": target},
            ).start()

        pltpu.make_async_copy(
            blocks_ref.at[me, part], arrived.at[part, me], volt_recv.at[part]
        ).start()

    stages = (
        (cores, lambda d: device(my_z, my_x, lax.rem(my_core + d, cores))),
        (width, lambda d: device(my_z, lax.rem(my_x + d, width), my_core)),
        (depth, lambda d: device(lax.rem(my_z + d, depth), my_x, my_core)),
    )
    total = pick_ref[...].astype(jnp.float32)
    base = 0
    for number, (extent, target) in enumerate(stages):
        if extent == 1:
            continue
        partial[number] = total.astype(jnp.bfloat16)
        copies = [
            remote(
                partial.at[number], slots.at[base + d - 1],
                steer_send.at[base + d - 1], steer_recv.at[base + d - 1], target(d),
            )
            for d in range(1, extent)
        ]
        for copy in copies:
            copy.start()
        if number == 0:
            start_volts(0)
        for copy in copies:
            copy.wait()
        for d in range(1, extent):
            total = total + slots[base + d - 1].astype(jnp.float32)
        base += extent - 1
    steer[...] = total

    def z_row(part):
        return gathered_ref.at[part, my_core, my_x]

    def start_z(part):
        for d in range(1, depth):
            remote(
                own_ref.at[part], gathered_ref.at[part, my_core, my_x, my_z],
                z_send.at[part], z_recv.at[part], device(lax.rem(my_z + d, depth), my_x, my_core),
            ).start()
        pltpu.make_async_copy(
            own_ref.at[part], gathered_ref.at[part, my_core, my_x, my_z], place_sem.at[part]
        ).start()

    def start_x(part):
        take(own_ref.at[part], place_sem.at[part])
        take(gathered_ref.at[part, my_core, my_x, pl.ds(0, depth - 1)], z_recv.at[part])
        for d in range(1, width):
            remote(
                z_row(part), z_row(part), x_send.at[part], x_recv.at[part],
                device(my_z, lax.rem(my_x + d, width), my_core),
            ).start()

    def start_core(part):
        take(gathered_ref.at[part, my_core, pl.ds(0, width - 1)], x_recv.at[part])
        for d in range(1, cores):
            remote(
                gathered_ref.at[part, my_core], gathered_ref.at[part, my_core],
                core_send.at[part], core_recv.at[part],
                device(my_z, my_x, lax.rem(my_core + d, cores)),
            ).start()

    @pl.loop(0, parts)
    def _(part):
        take(arrived.at[part], volt_recv.at[part])

        @pl.when(part + 1 < parts)
        def _():
            start_volts(part + 1)

        compute_part(
            part, arrived, mask_ref, count_ref, steer, own_ref,
            (real_hi, real_lo, imag_hi, imag_lo),
        )
        start_z(part)

        @pl.when(part >= 1)
        def _():
            start_x(part - 1)

        @pl.when(part >= 2)
        def _():
            start_core(part - 2)

    if parts >= 2:
        start_core(parts - 2)
    start_x(parts - 1)
    start_core(parts - 1)

    @pl.loop(0, parts)
    def _(part):
        take(gathered_ref.at[part, pl.ds(0, cores - 1)], core_recv.at[part])
        take(arrived.at[part, pl.ds(0, devices - 1)], volt_send.at[part])
        take(gathered_ref.at[part, my_core, my_x, pl.ds(0, depth - 1)], z_send.at[part])
        take(gathered_ref.at[part, my_core, pl.ds(0, width - 1)], x_send.at[part])
        take(gathered_ref.at[part, pl.ds(0, cores - 1)], core_send.at[part])


def exchange(dims, chans, blocks, pick, mask, count):
    depth, width, cores = dims
    devices, parts, rows_dev, double = blocks.shape
    ports = double // 2
    beams2 = pick.shape[0]
    rows = chans * beams2 // 2
    hops = depth + width + cores - 3
    bf16, dma = jnp.bfloat16, pltpu.SemaphoreType.DMA
    vmem = pl.BlockSpec(memory_space=pltpu.VMEM)
    anywhere = pl.BlockSpec(memory_space=pl.ANY)
    return pl.pallas_call(
        functools.partial(exchange_kernel, dims),
        out_shape=(
            jax.ShapeDtypeStruct((parts, cores, width, depth, rows, double), bf16),
            jax.ShapeDtypeStruct((parts, rows, double), bf16),
        ),
        in_specs=[anywhere, vmem, vmem, vmem],
        out_specs=(anywhere, vmem),
        scratch_shapes=[
            pltpu.VMEM((parts, devices, rows_dev, double), bf16),
            pltpu.VMEM((hops, beams2, ports), bf16),
            pltpu.VMEM((3, beams2, ports), bf16),
            pltpu.VMEM((beams2, ports), jnp.float32),
        ]
        + [pltpu.VMEM((chans, ports, ports), bf16)] * 4
        + [dma((parts,)), dma((parts,)), dma((hops,)), dma((hops,))]
        + [dma((parts,))] * 7,
        compiler_params=pltpu.CompilerParams(
            collective_id=0, has_side_effects=True, vmem_limit_bytes=40 * 1024 * 1024
        ),
    )(blocks, pick, mask, count)


def map_kernel(beams, weights_ref, pattern_ref, out_ref):
    parts, _, _, _, rows, double = weights_ref.shape
    chans = out_ref.shape[1] // parts
    pixels = pattern_ref.shape[1] // 2
    flat = weights_ref[:, 0, 0, 0].reshape(parts * rows, double)
    response = dot32(flat, pattern_ref[...])
    real, imag = response[:, :pixels], response[:, pixels:]
    power = (real * real + imag * imag).reshape(parts * chans, rows // chans, pixels)
    out_ref[0] = power[:, :beams]


def beam_power(dims, chans, gathered, patterns, beams):
    depth, width, cores = dims
    parts, _, _, _, rows, double = gathered.shape
    pixels = patterns.shape[1] // 2
    senders = depth * width * cores
    return pl.pallas_call(
        functools.partial(map_kernel, beams),
        grid=(senders,),
        out_shape=jax.ShapeDtypeStruct((senders, parts * chans, beams, pixels), jnp.float32),
        in_specs=[
            pl.BlockSpec(
                (parts, 1, 1, 1, rows, double),
                lambda i: (0, i % cores, (i // cores) % width, i // (cores * width), 0, 0),
            ),
            pl.BlockSpec((double, 2 * pixels), lambda i: (0, 0)),
        ],
        out_specs=pl.BlockSpec((1, parts * chans, beams, pixels), lambda i: (i, 0, 0, 0)),
        compiler_params=pltpu.CompilerParams(vmem_limit_bytes=32 * 1024 * 1024),
    )(gathered, patterns)


def torus_dims(devices):
    cores = 2 if devices % 2 == 0 else 1
    chips = devices // cores
    width = 1
    while chips % (4 * width * width) == 0:
        width *= 2
    return chips // width, width, cores


def on_device(voltages, off_starts, pointing, patterns):
    devices = lax.axis_size("tm")
    position = lax.axis_index("tm")
    channels, samples_dev, _, ports = voltages.shape
    beams = pointing.shape[0]
    padded = -(-beams // 8) * 8
    per_dev = channels // devices
    parts = 4 if per_dev % 4 == 0 else 1
    chans = per_dev // parts
    dims = torus_dims(devices)
    total_time = samples_dev * devices
    off_span = max(4, total_time // 32)
    is_off = off_flags(jnp.arange(total_time, dtype=jnp.int32), off_starts, off_span)
    off_count = jnp.sum(is_off.astype(jnp.float32))
    count = jnp.broadcast_to(off_count, (1, ports))
    mask = jnp.broadcast_to((~is_off)[:, None], (total_time, ports)).astype(jnp.float32)
    pixels = patterns.shape[2]
    pixel_ids = position * pixels + jnp.arange(pixels, dtype=jnp.int32)
    wanted = jnp.pad(pointing, (0, padded - beams), constant_values=-1)
    selector = (wanted[:, None] == pixel_ids[None, :]).astype(jnp.bfloat16)
    picked = jnp.einsum("rpx,bx->rbp", patterns, selector, preferred_element_type=jnp.float32)
    picked = picked.astype(jnp.bfloat16).reshape(2 * padded, ports)
    blocks = voltages.reshape(devices, parts, chans * samples_dev, 2 * ports)
    pattern_rows = jnp.concatenate(
        [
            jnp.concatenate([patterns[0], patterns[1]], axis=1),
            jnp.concatenate([patterns[1], -patterns[0]], axis=1),
        ],
        axis=0,
    )
    gathered, own = exchange(dims, chans, blocks, picked, mask, count)
    maps = beam_power(dims, chans, gathered, pattern_rows, beams)
    own = own.reshape(per_dev, padded, 2, ports)[:, :beams].transpose(0, 2, 1, 3)
    return (
        own.reshape(per_dev, 2, beams * ports),
        maps.reshape(channels, beams, pixels),
    )


def solution(mesh):
    in_specs = (P(None, ("groups", "tm"), None, None), P("groups"), P(), P(None, None, "tm"))
    out_specs = (P(("groups", "tm"), None, None), P("groups", None, "tm"))
    return jax.shard_map(
        on_device, mesh=mesh, in_specs=in_specs, out_specs=out_specs, check_vma=False
    )
```

```python
import functools
import jax
import jax.numpy as jnp
from jax import lax
from jax.experimental import pallas as pl
from jax.experimental.pallas import tpu as pltpu
from jax.sharding import PartitionSpec as P

ITERS = 20
MESH = pl.DeviceIdType.MESH


def off_flags(moments, starts, range_len):
    inside = (moments[None, :] >= starts[:, None]) & (
        moments[None, :] < starts[:, None] + range_len
    )
    return jnp.any(inside, axis=0)


def split_two(value):
    high = value.astype(jnp.bfloat16)
    return high, (value - high.astype(jnp.float32)).astype(jnp.bfloat16)


def dot32(a, b):
    return jnp.dot(a, b, preferred_element_type=jnp.float32)


def correlate(volt_ref, part, c, mask, count):
    senders, rows_dev, width = volt_ref.shape[1:]
    ports = width // 2
    samples_dev = mask.shape[0] // senders
    wide = volt_ref[part].astype(jnp.float32)
    wide = wide[:, c * samples_dev : (c + 1) * samples_dev].reshape(senders * samples_dev, width)
    first, second = wide[:, :ports], wide[:, ports:]
    on_first, on_second = first * mask, second * mask
    power = (first * first + second * second) * (1.0 - mask)
    noise_power = jnp.sum(power, axis=0, keepdims=True) / count + 1e-06
    pair = jnp.concatenate([first, second], axis=0).astype(jnp.bfloat16)
    on_pair = jnp.concatenate([on_first, on_second], axis=0).astype(jnp.bfloat16)
    turned = jnp.concatenate([on_second, -on_first], axis=0).astype(jnp.bfloat16)
    dims = (((0,), (0,)), ((), ()))
    corr_real = lax.dot_general(on_pair, pair, dims, preferred_element_type=jnp.float32)
    corr_imag = lax.dot_general(turned, pair, dims, preferred_element_type=jnp.float32)
    return corr_real, corr_imag, 1.0 / noise_power


def compute_part(part, volt_ref, mask_ref, count_ref, steer_ref, out_ref, stage, mats):
    real_hi, real_lo, imag_hi, imag_lo = mats
    chans = real_hi.shape[0]
    ports = real_hi.shape[1]
    beams = steer_ref.shape[0] // 2
    steer_real = steer_ref[:beams]
    steer_imag = steer_ref[beams:]
    gain = steer_real * steer_real + steer_imag * steer_imag
    inverse_noise = []
    for c in range(chans):
        corr_real, corr_imag, inverse = correlate(
            volt_ref, part, c, mask_ref[...], count_ref[...]
        )
        inverse_noise.append(inverse)
        real_hi[c], real_lo[c] = split_two(corr_real)
        imag_hi[c], imag_lo[c] = split_two(corr_imag)

    def mix(c, state):
        high, low = split_two(state)
        both = jnp.concatenate([high, low], axis=0)
        by_real = dot32(both, real_hi[c])
        by_imag = dot32(both, imag_hi[c])
        by_real = by_real[: 2 * beams] + by_real[2 * beams :] + dot32(high, real_lo[c])
        by_imag = by_imag[: 2 * beams] + by_imag[2 * beams :] + dot32(high, imag_lo[c])
        return by_real[:beams] + by_imag[beams:], by_real[beams:] - by_imag[:beams]

    weighting = [gain * inv for inv in inverse_noise]

    def power_turn(counter, states):
        new_states = []
        for c in range(chans):
            mixed_real, mixed_imag = mix(c, states[c])
            next_real = weighting[c] * mixed_real
            next_imag = weighting[c] * mixed_imag
            total = jnp.sum(
                next_real * mixed_real + next_imag * mixed_imag, axis=1, keepdims=True
            )
            factor = lax.rsqrt(total / (2 * ports) + 1e-06)
            new_states.append(jnp.concatenate([next_real * factor, next_imag * factor], axis=0))
        return tuple(new_states)

    states = tuple(
        jnp.concatenate([gain * jnp.sqrt(inv), jnp.zeros_like(gain)], axis=0)
        for inv in inverse_noise
    )
    states = lax.fori_loop(0, ITERS - 1, power_turn, states)
    beam_rows = stage.shape[0] // chans
    for c in range(chans):
        mixed_real, mixed_imag = mix(c, states[c])
        total = jnp.sum(
            weighting[c] * mixed_real * mixed_real + weighting[c] * mixed_imag * mixed_imag,
            axis=1,
            keepdims=True,
        )
        factor = lax.rsqrt(total / (2 * ports) + 1e-06) * inverse_noise[c]
        weight_real = (steer_real * mixed_real - steer_imag * mixed_imag) * factor
        weight_imag = (steer_real * mixed_imag + steer_imag * mixed_real) * factor
        both = jnp.concatenate([weight_real, weight_imag], axis=1)
        stage[c * beam_rows : (c + 1) * beam_rows] = both[:beam_rows]
    out_ref[part] = stage[...].astype(jnp.bfloat16)


def exchange_kernel(
    dims, blocks_ref, pick_ref, mask_ref, count_ref, gathered_ref, own_ref,
    arrived, slots, partial, steer, stage, real_hi, real_lo, imag_hi, imag_lo,
    volt_send, volt_recv, steer_send, steer_recv,
    z_send, z_recv, x_send, x_recv, core_send, core_recv, place_sem,
):
    depth, width, cores = dims
    devices = depth * width * cores
    parts = arrived.shape[0]
    me = lax.axis_index("tm")
    my_core = lax.rem(me, cores)
    my_x = lax.rem(me // cores, width)
    my_z = me // (cores * width)

    def device(z, x, core):
        return {"tm": (z * width + x) * cores + core}

    def remote(src, dst, send, recv, target):
        return pltpu.make_async_remote_copy(
            src_ref=src, dst_ref=dst, send_sem=send, recv_sem=recv,
            device_id=target, device_id_type=MESH,
        )

    def take(ref, sem):
        pltpu.make_async_copy(ref, ref, sem).wait()

    barrier = pltpu.get_barrier_semaphore()

    @pl.loop(1, devices)
    def _(step):
        pl.semaphore_signal(
            barrier, inc=1, device_id={"tm": lax.rem(me + step, devices)}, device_id_type=MESH
        )

    pl.semaphore_wait(barrier, devices - 1)

    def start_volts(part):
        @pl.loop(1, devices)
        def _(step):
            target = lax.rem(me + step, devices)
            remote(
                blocks_ref.at[target, part], arrived.at[part, me],
                volt_send.at[part], volt_recv.at[part], {"tm": target},
            ).start()

        pltpu.make_async_copy(
            blocks_ref.at[me, part], arrived.at[part, me], volt_recv.at[part]
        ).start()

    stages = (
        (cores, lambda d: device(my_z, my_x, lax.rem(my_core + d, cores))),
        (width, lambda d: device(my_z, lax.rem(my_x + d, width), my_core)),
        (depth, lambda d: device(lax.rem(my_z + d, depth), my_x, my_core)),
    )
    total = pick_ref[...].astype(jnp.float32)
    base = 0
    for number, (extent, target) in enumerate(stages):
        if extent == 1:
            continue
        partial[number] = total.astype(jnp.bfloat16)
        copies = [
            remote(
                partial.at[number], slots.at[base + d - 1],
                steer_send.at[base + d - 1], steer_recv.at[base + d - 1], target(d),
            )
            for d in range(1, extent)
        ]
        for copy in copies:
            copy.start()
        if number == 0:
            start_volts(0)
        for copy in copies:
            copy.wait()
        for d in range(1, extent):
            total = total + slots[base + d - 1].astype(jnp.float32)
        base += extent - 1
    steer[...] = total
    if parts > 1:
        start_volts(1)

    def slot(part, z):
        return gathered_ref.at[part, my_core, my_x, z]

    def to_x(part, source, z):
        for d in range(1, width):
            remote(
                source, slot(part, z), x_send.at[part], x_recv.at[part],
                device(my_z, lax.rem(my_x + d, width), my_core),
            ).start()

    def start_z(part):
        for d in range(1, depth):
            remote(
                own_ref.at[part], slot(part, my_z), z_send.at[part], z_recv.at[part, d],
                device(lax.rem(my_z + d, depth), my_x, my_core),
            ).start()
        to_x(part, own_ref.at[part], my_z)
        pltpu.make_async_copy(own_ref.at[part], slot(part, my_z), place_sem.at[part]).start()

    def start_x(part):
        take(own_ref.at[part], place_sem.at[part])
        for d in range(1, depth):
            z = lax.rem(my_z + depth - d, depth)
            take(slot(part, z), z_recv.at[part, d])
            to_x(part, slot(part, z), z)

    def start_core(part):
        take(gathered_ref.at[part, my_core, pl.ds(0, width - 1)], x_recv.at[part])
        for d in range(1, cores):
            remote(
                gathered_ref.at[part, my_core], gathered_ref.at[part, my_core],
                core_send.at[part], core_recv.at[part],
                device(my_z, my_x, lax.rem(my_core + d, cores)),
            ).start()

    @pl.loop(0, parts)
    def _(part):
        take(arrived.at[part], volt_recv.at[part])

        @pl.when(part + 2 < parts)
        def _():
            start_volts(part + 2)

        compute_part(
            part, arrived, mask_ref, count_ref, steer, own_ref, stage,
            (real_hi, real_lo, imag_hi, imag_lo),
        )
        start_z(part)

        @pl.when(part >= 1)
        def _():
            start_x(part - 1)

        @pl.when(part >= 2)
        def _():
            start_core(part - 2)

    if parts >= 2:
        start_core(parts - 2)
    start_x(parts - 1)
    start_core(parts - 1)

    @pl.loop(0, parts)
    def _(part):
        take(gathered_ref.at[part, pl.ds(0, cores - 1)], core_recv.at[part])
        take(arrived.at[part, pl.ds(0, devices - 1)], volt_send.at[part])
        take(gathered_ref.at[part, my_core, my_x, pl.ds(0, depth - 1)], z_send.at[part])
        take(gathered_ref.at[part, my_core, pl.ds(0, width - 1)], x_send.at[part])
        take(gathered_ref.at[part, pl.ds(0, cores - 1)], core_send.at[part])


def exchange(dims, chans, beam_rows, blocks, pick, mask, count):
    depth, width, cores = dims
    devices, parts, rows_dev, double = blocks.shape
    ports = double // 2
    beams2 = pick.shape[0]
    rows = chans * beam_rows
    hops = depth + width + cores - 3
    bf16, dma = jnp.bfloat16, pltpu.SemaphoreType.DMA
    vmem = pl.BlockSpec(memory_space=pltpu.VMEM)
    anywhere = pl.BlockSpec(memory_space=pl.ANY)
    return pl.pallas_call(
        functools.partial(exchange_kernel, dims),
        out_shape=(
            jax.ShapeDtypeStruct((parts, cores, width, depth, rows, double), bf16),
            jax.ShapeDtypeStruct((parts, rows, double), bf16),
        ),
        in_specs=[anywhere, vmem, vmem, vmem],
        out_specs=(anywhere, vmem),
        scratch_shapes=[
            pltpu.VMEM((parts, devices, rows_dev, double), bf16),
            pltpu.VMEM((hops, beams2, ports), bf16),
            pltpu.VMEM((3, beams2, ports), bf16),
            pltpu.VMEM((beams2, ports), jnp.float32),
            pltpu.VMEM((rows, double), jnp.float32),
        ]
        + [pltpu.VMEM((chans, ports, ports), bf16)] * 4
        + [dma((parts,)), dma((parts,)), dma((hops,)), dma((hops,))]
        + [dma((parts,)), dma((parts, depth))] + [dma((parts,))] * 5,
        compiler_params=pltpu.CompilerParams(
            collective_id=0, has_side_effects=True, vmem_limit_bytes=56 * 1024 * 1024
        ),
    )(blocks, pick, mask, count)


def map_kernel(weights_ref, pattern_ref, out_ref, power):
    parts, _, _, _, rows, double = weights_ref.shape
    beams, _, chans, pixels = out_ref.shape
    stride = parts * rows // chans
    flat = weights_ref[:, 0, 0, 0].reshape(parts * rows, double)
    response = dot32(flat, pattern_ref[...])
    real, imag = response[:, :pixels], response[:, pixels:]
    power[...] = real * real + imag * imag
    for b in range(beams):
        out_ref[b, 0] = power[pl.ds(b, chans, stride=stride), :]


def beam_power(dims, chans, gathered, patterns, beams):
    depth, width, cores = dims
    parts, _, _, _, rows, double = gathered.shape
    pixels = patterns.shape[1] // 2
    senders = depth * width * cores
    per_dev = parts * chans
    return pl.pallas_call(
        map_kernel,
        grid=(senders,),
        out_shape=jax.ShapeDtypeStruct((beams, senders, per_dev, pixels), jnp.float32),
        in_specs=[
            pl.BlockSpec(
                (parts, 1, 1, 1, rows, double),
                lambda i: (0, i % cores, (i // cores) % width, i // (cores * width), 0, 0),
            ),
            pl.BlockSpec((double, 2 * pixels), lambda i: (0, 0)),
        ],
        out_specs=pl.BlockSpec((beams, 1, per_dev, pixels), lambda i: (0, i, 0, 0)),
        scratch_shapes=[pltpu.VMEM((parts * rows, pixels), jnp.float32)],
        compiler_params=pltpu.CompilerParams(vmem_limit_bytes=56 * 1024 * 1024),
    )(gathered, patterns)


def torus_dims(devices):
    cores = 2 if devices % 2 == 0 else 1
    chips = devices // cores
    width = 1
    while chips % (4 * width * width) == 0:
        width *= 2
    return chips // width, width, cores


def on_device(voltages, off_starts, pointing, patterns):
    devices = lax.axis_size("tm")
    position = lax.axis_index("tm")
    channels, samples_dev, _, ports = voltages.shape
    beams = pointing.shape[0]
    padded = -(-beams // 8) * 8
    per_dev = channels // devices
    parts = 4 if per_dev % 4 == 0 else 1
    chans = per_dev // parts
    dims = torus_dims(devices)
    beam_rows = beams if (chans * beams) % 16 == 0 else padded
    total_time = samples_dev * devices
    off_span = max(4, total_time // 32)
    is_off = off_flags(jnp.arange(total_time, dtype=jnp.int32), off_starts, off_span)
    off_count = jnp.sum(is_off.astype(jnp.float32))
    count = jnp.broadcast_to(off_count, (1, ports))
    mask = jnp.broadcast_to((~is_off)[:, None], (total_time, ports)).astype(jnp.float32)
    pixels = patterns.shape[2]
    pixel_ids = position * pixels + jnp.arange(pixels, dtype=jnp.int32)
    wanted = jnp.pad(pointing, (0, padded - beams), constant_values=-1)
    selector = (wanted[:, None] == pixel_ids[None, :]).astype(jnp.bfloat16)
    picked = jnp.einsum("rpx,bx->rbp", patterns, selector, preferred_element_type=jnp.float32)
    picked = picked.astype(jnp.bfloat16).reshape(2 * padded, ports)
    blocks = voltages.reshape(devices, parts, chans * samples_dev, 2 * ports)
    pattern_rows = jnp.concatenate(
        [
            jnp.concatenate([patterns[0], patterns[1]], axis=1),
            jnp.concatenate([patterns[1], -patterns[0]], axis=1),
        ],
        axis=0,
    )
    gathered, own = exchange(dims, chans, beam_rows, blocks, picked, mask, count)
    maps = beam_power(dims, chans, gathered, pattern_rows, beams)
    own = own.reshape(per_dev, beam_rows, 2, ports)[:, :beams].transpose(0, 2, 1, 3)
    return (
        own.reshape(per_dev, 2, beams * ports),
        maps.reshape(beams, channels, pixels).transpose(1, 0, 2),
    )


def solution(mesh):
    in_specs = (P(None, ("groups", "tm"), None, None), P("groups"), P(), P(None, None, "tm"))
    out_specs = (P(("groups", "tm"), None, None), P("groups", None, "tm"))
    return jax.shard_map(
        on_device, mesh=mesh, in_specs=in_specs, out_specs=out_specs, check_vma=False
    )
```
